512 devices in a mesh: pipe: 64 (over x, z), tp: 8 (over y, core).
Axes of the slice: x: 4, y: 4, z: 16, core: 2. Of those that a mesh axis runs over, the one named last changes fastest.
Arguments:
- attn_out: bfloat16 [512, 8192], P('pipe', 'tp'), may hold values from -6 to 6
- residual: bfloat16 [512, 8192], P(None, 'pipe'), may hold values from -6 to 6
- o_weight: bfloat16 [8192, 8192], P('tp', 'pipe'), may hold values from -0.0625 to 0.0625
- norm_gain: float32 [8192], P('pipe'), may hold values from 0.5 to 1.5
- head_weight: bfloat16 [8192, 131072], P(None, ('pipe', 'tp')), may hold values from -127 to 127, as said below
- head_scale: float32 [131072], P(('pipe', 'tp')), may hold values from 0.00025 to 0.0009
- policy_logits: bfloat16 [512, 131072], P(None, ('pipe', 'tp')), may hold values from -300 to 300
- token_ids: int32 [512], replicated, may hold values from 0 to 131071
- lengths: int32 [8], replicated, may hold values from 1 to 64, as said below
- loss_mask: int32 [512], replicated, may hold values 0 or 1
Outputs:
- grad_policy: bfloat16 [512, 131072], P(None, ('pipe', 'tp'))
- token_logprob: float32 [512], replicated
- kl_token: float32 [512], replicated
The draws below stay inside these ranges and needn't reach their ends.
Inputs may be any that keep to these rules, and one draw needn't show every extreme that they name: `head_weight`: whole numbers, int8 codes held in bfloat16. `lengths`: some response has all 64 positions.
All inputs are finite; a program needn't handle non-finite values.
Results may differ from the reference program's by a relative error of at most 0.012.
Values may be sent and summed in bfloat16 or wider, within the bound.
No kernel may reach another device: no remote copies, remote signals or barrier semaphores. Data moves between devices by JAX's collectives and lax.ppermute only.
A program may use at most 64 MiB of HBM per device.

```python
import math
import jax
import jax.numpy as jnp
import numpy as np
from jax import lax

D = 8192
HEADS = 64
HEAD_DIM = 128
RESP = 64
TOKENS = 512
VOCAB = 131072
SEQS = 8


def draw_residual(key, part):
    key = jax.random.fold_in(key, 3)
    values = jnp.clip(jax.random.normal(key, (TOKENS, D), jnp.float32), -6.0, 6.0)
    return values.astype(jnp.bfloat16)


def draw_head_weight(key, part):
    key = jax.random.fold_in(key, 7)
    codes = jax.random.randint(key, (D, VOCAB), -127, 128).astype(jnp.float32)
    return codes.astype(jnp.bfloat16)


def draw_head_scale(key, part):
    key = jax.random.fold_in(key, 13)
    logs = jax.random.uniform(key, (VOCAB,), jnp.float32, math.log(0.00025), math.log(0.0009))
    values = jnp.clip(jnp.exp(logs), 0.00025, 0.0009)
    return values.astype(jnp.float32)


def draw_policy_logits(key, part):
    key = jax.random.fold_in(key, 11)
    values = jnp.clip(3.0 * jax.random.normal(key, (TOKENS, VOCAB), jnp.float32), -18.0, 18.0)
    return values.astype(jnp.bfloat16)


def draw_lengths(key, part):
    key = jax.random.fold_in(key, 5)
    values = jax.random.randint(key, (SEQS,), 1, RESP + 1)
    chosen = jax.random.randint(jax.random.fold_in(key, 1), (), 0, SEQS)
    return jnp.where(jnp.arange(SEQS, dtype=jnp.int32) == chosen, RESP, values).astype(jnp.int32)


def touch_ends(array, rng, smallest, largest):
    place = [jax.random.randint(jax.random.fold_in(rng, axis), (), 0, length) for axis, length in enumerate(array.shape)]
    main_axis = array.shape.index(max(array.shape))
    beside = place[:main_axis] + [(place[main_axis] + 1) % array.shape[main_axis]] + place[main_axis + 1:]
    return array.at[tuple(place)].set(smallest).at[tuple(beside)].set(largest)


def block_scale(rng, dims, pieces, least, high):
    loudness, own = 1.0, jax.random.fold_in(rng, 6)
    for position, parts in pieces:
        draws = jnp.exp(jax.random.uniform(jax.random.fold_in(own, position), (parts,), jnp.float32, least / len(pieces), high / len(pieces)))
        loudness = loudness * jnp.repeat(draws, dims[position] // parts).reshape([-1 if axis == position else 1 for axis in range(len(dims))])
    return loudness


def wide_ids(own_key, dims, count, lean):
    portions = [min(1 << octave, count + 1 - (1 << octave)) * (1 << 20) // math.isqrt((1 << octave) ** lean) + 1 for octave in range((count + 1).bit_length()) if 1 << octave <= count]
    spread = 1 + sum(portions) // (1 << 30)
    table = np.cumsum(np.array([max(1, weight // spread) for weight in portions]))
    pick = jax.random.randint(jax.random.fold_in(own_key, 1), dims, 0, int(table[len(portions) - 1]))
    start = jnp.left_shift(1, jnp.searchsorted(jnp.asarray(table, jnp.int32), pick, side="right").astype(jnp.int32))
    grade = start - 1 + jax.random.randint(jax.random.fold_in(own_key, 4), dims, 0, 1 << 30) % jnp.minimum(start, count + 1 - start)
    return jax.random.permutation(jax.random.fold_in(own_key, 2), count)[grade].astype(jnp.int32)


def normal_values(own_key, shape, scale, reach, cuts=(), kind=jnp.bfloat16):
    factor_of = block_scale(own_key, shape, cuts, -0.22, 0.18) if cuts else 1.0
    values = jax.random.normal(own_key, shape, jnp.float32) * scale * factor_of
    return jnp.minimum(jnp.maximum(values, -reach), reach).astype(kind)


def setup_inputs(seed: int = 0) -> dict:
    splits = jax.random.split(jax.random.key(seed), 11)
    return {
        "attn_out": normal_values(splits[0], (TOKENS, HEADS * HEAD_DIM), 1.0, 6.0, ((0, 64), (1, 8))),
        "residual": draw_residual(jax.random.fold_in(splits[10], 71), 0),
        "o_weight": normal_values(splits[2], (HEADS * HEAD_DIM, D), (HEADS * HEAD_DIM) ** -0.5, 0.0625, ((0, 8), (1, 64))),
        "norm_gain": jnp.clip(1.0 + 0.1 * jax.random.normal(splits[3], (D,), jnp.float32), 0.5, 1.5),
        "head_weight": draw_head_weight(jax.random.fold_in(splits[10], 71), 0),
        "head_scale": draw_head_scale(jax.random.fold_in(splits[10], 71), 0),
        "policy_logits": draw_policy_logits(jax.random.fold_in(splits[10], 71), 0),
        "token_ids": touch_ends(wide_ids(splits[7], (TOKENS,), VOCAB, 2), jax.random.fold_in(splits[7], 3), 0, VOCAB - 1).astype(jnp.int32),
        "lengths": draw_lengths(jax.random.fold_in(splits[10], 71), 0),
        "loss_mask": touch_ends((jax.random.randint(splits[9], (TOKENS,), 0, 8) < 7).astype(jnp.int32), jax.random.fold_in(splits[9], 1), 0, 1),
    }


def log_total(logits):
    top = lax.optimization_barrier(jnp.max(logits, axis=1))
    return top + jnp.log(lax.optimization_barrier(jnp.sum(jnp.exp(logits - top[:, None]), axis=1)))

def reference(attn_out, residual, o_weight, norm_gain, head_weight, head_scale, policy_logits, token_ids, lengths, loss_mask):
    projected = jnp.dot(attn_out, o_weight, preferred_element_type=jnp.float32)
    stream = residual.astype(jnp.float32) + projected
    row_scale = lax.rsqrt(lax.optimization_barrier(jnp.sum(stream * stream, axis=1, keepdims=True)) / D + 1e-06)
    hidden = (stream * row_scale * norm_gain[None, :]).astype(jnp.bfloat16)
    ref_logits = jnp.dot(hidden, head_weight, preferred_element_type=jnp.float32) * head_scale[None, :]
    policy = policy_logits.astype(jnp.float32)
    ref_lse = log_total(ref_logits)
    policy_lse = log_total(policy)
    ref_logp = ref_logits - ref_lse[:, None]
    policy_logp = policy - policy_lse[:, None]
    probs = jnp.exp(policy_logp)
    kl_raw = lax.optimization_barrier(jnp.sum(probs * (policy_logp - ref_logp), axis=1))
    positions = jnp.arange(TOKENS, dtype=jnp.int32)
    seq_len = lengths[positions // RESP]
    live = jnp.where((positions % RESP < seq_len) & (loss_mask > 0), 1.0, 0.0).astype(jnp.float32)
    picked = jnp.take_along_axis(ref_logits, token_ids[:, None].astype(jnp.int32), axis=1)[:, 0]
    token_logprob = picked - ref_lse
    kl_token = live * kl_raw
    grad_policy = (live[:, None] * probs * (policy_logp - ref_logp - kl_raw[:, None])).astype(jnp.bfloat16)
    return (grad_policy, token_logprob, kl_token)
```

```python
import jax
import jax.numpy as jnp
from jax import lax
from jax.sharding import Mesh, PartitionSpec as P

D = 8192
RESP = 64
NX, NZ, NY, NC = 4, 16, 4, 2
PIPE = ("x", "z")
TP = ("y", "c")
VOC = ("x", "z", "y", "c")
BF16, F32 = jnp.bfloat16, jnp.float32


def share(block, axes, count):
    return lax.all_to_all(jnp.broadcast_to(block[None], (count,) + block.shape), axes, 0, 0)


def pieces(value):
    high = lax.reduce_precision(value, 8, 7)
    mid = lax.reduce_precision(value - high, 8, 7)
    low = value - high - mid
    return high.astype(BF16), mid.astype(BF16), low.astype(BF16)


def join(high, mid, low):
    return high.astype(F32) + mid.astype(F32) + low.astype(F32)


def swap_cores(value):
    return lax.ppermute(value, "c", [(0, 1), (1, 0)])


def combine(stats):
    ref_max, policy_max = stats[:, 0], stats[:, 1]
    ref_top, policy_top = jnp.max(ref_max, axis=0), jnp.max(policy_max, axis=0)
    ref_down, policy_down = ref_max - ref_top, policy_max - policy_top
    ref_factor, policy_factor = jnp.exp(ref_down), jnp.exp(policy_down)
    ref_sum = jnp.sum(stats[:, 2] * ref_factor, axis=0)
    policy_sum = jnp.sum(stats[:, 3] * policy_factor, axis=0)
    weighted = jnp.sum(
        (stats[:, 4] + stats[:, 3] * (policy_down - ref_down)) * policy_factor, axis=0
    )
    picked = jnp.sum(stats[:, 5], axis=0)
    return jnp.stack([ref_top, policy_top, ref_sum, policy_sum, weighted, picked])


def on_device(
    attn_out,
    residual,
    o_weight,
    norm_gain,
    head_weight,
    head_scale,
    policy_logits,
    token_ids,
    lengths,
    loss_mask,
):
    y, c = lax.axis_index("y"), lax.axis_index("c")
    tokens = residual.shape[0]
    rows_x = tokens // NX
    rows = rows_x // NY
    cols = o_weight.shape[1]
    depth = o_weight.shape[0]
    half = D // NC
    vocab_dev = head_weight.shape[1]

    own_weight = lax.dynamic_slice_in_dim(head_weight, c * half, half, 0)
    peer_weight = swap_cores(lax.dynamic_slice_in_dim(head_weight, (1 - c) * half, half, 0))

    attn = share(attn_out, "z", NZ).reshape(rows_x, depth)
    gain_rows = jnp.concatenate(
        [jnp.stack(pieces(norm_gain)), jnp.zeros((13, cols), BF16)]
    )
    to_x = jnp.concatenate(
        [
            jnp.broadcast_to(o_weight[None], (NX, depth, cols)),
            residual.reshape(NX, rows_x, cols),
            jnp.broadcast_to(gain_rows[None], (NX, 16, cols)),
        ],
        axis=1,
    )
    from_x = lax.all_to_all(to_x, "x", 0, 0)
    terms = jnp.stack(
        [
            jnp.dot(attn, from_x[i, :depth], preferred_element_type=F32)
            for i in range(NX)
        ]
    )
    terms = terms.reshape(NC, NX // NC, NY, rows, cols).transpose(2, 0, 1, 3, 4)
    terms = lax.all_to_all(terms.reshape(NY * NC, NX // NC, rows, cols), TP, 0, 0)
    own_from = lax.dynamic_slice_in_dim(from_x, c * (NX // NC), NX // NC, 0)
    own_residual = lax.dynamic_slice_in_dim(
        own_from[:, depth : depth + rows_x], y * rows, rows, 1
    )
    gain = join(*(own_from[:, depth + rows_x + i] for i in range(3)))
    stream = own_residual.astype(F32) + jnp.sum(terms, axis=0)
    squares = jnp.sum(stream * stream, axis=(0, 2))
    scaled = (stream * gain[:, None, :]).astype(BF16)

    square_rows = jnp.concatenate(
        [jnp.concatenate(pieces(squares)), jnp.zeros((cols - 3 * rows,), BF16)]
    )
    to_z = jnp.concatenate(
        [
            scaled.reshape(NX // NC * rows, cols),
            jnp.broadcast_to(square_rows[None], (16, cols)),
        ]
    )
    from_z = share(to_z, "z", NZ)
    features = from_z[:, : NX // NC * rows].reshape(NZ, NX // NC, rows, cols)
    features = features.transpose(2, 1, 0, 3).reshape(rows, half)
    square_z = from_z[:, NX // NC * rows]
    squares = jnp.sum(
        join(*(square_z[:, i * rows : (i + 1) * rows] for i in range(3))), axis=0
    )
    square_cols = jnp.concatenate(
        [jnp.stack(pieces(squares), axis=1), jnp.zeros((rows, 125), BF16)], axis=1
    )
    hidden = share(
        jnp.concatenate([features, square_cols], axis=1), ("x", "y"), NX * NY
    ).reshape(tokens, half + 128)
    squares = join(*(hidden[:, half + i] for i in range(3)))
    squares = squares + swap_cores(squares)
    hidden = hidden[:, :half]
    peer_logits = swap_cores(jnp.dot(hidden, peer_weight, preferred_element_type=F32))
    raw_logits = jnp.dot(hidden, own_weight, preferred_element_type=F32) + peer_logits
    row_scale = lax.rsqrt(squares / D + 1e-06)
    ref_logits = raw_logits * row_scale[:, None] * head_scale[None, :]

    policy = policy_logits.astype(F32)
    columns = lax.axis_index(VOC) * vocab_dev + jnp.arange(vocab_dev, dtype=jnp.int32)
    picked = jnp.sum(
        jnp.where(token_ids[:, None] == columns[None, :], ref_logits, 0.0), axis=1
    )
    ref_max, policy_max = jnp.max(ref_logits, axis=1), jnp.max(policy, axis=1)
    ref_down = ref_logits - ref_max[:, None]
    policy_down = policy - policy_max[:, None]
    policy_exp = jnp.exp(policy_down)
    stats = jnp.stack(
        [
            ref_max,
            policy_max,
            jnp.sum(jnp.exp(ref_down), axis=1),
            jnp.sum(policy_exp, axis=1),
            jnp.sum(policy_exp * (policy_down - ref_down), axis=1),
            picked,
        ]
    )
    stats = combine(share(stats, ("x", "y", "c"), NX * NY * NC))
    stats = combine(share(stats, "z", NZ))
    ref_log, policy_log = jnp.log(stats[2]), jnp.log(stats[3])
    ref_lse, policy_lse = stats[0] + ref_log, stats[1] + policy_log
    kl_raw = stats[4] / stats[3] - policy_log + ref_log

    positions = jnp.arange(tokens, dtype=jnp.int32)
    slots = jnp.arange(lengths.shape[0], dtype=jnp.int32)
    seq_len = jnp.sum(
        jnp.where((positions // RESP)[:, None] == slots[None, :], lengths[None, :], 0), axis=1
    )
    live = jnp.where((positions % RESP < seq_len) & (loss_mask > 0), 1.0, 0.0).astype(F32)
    ref_logp = ref_logits - ref_lse[:, None]
    policy_logp = policy - policy_lse[:, None]
    grad_policy = (
        live[:, None] * jnp.exp(policy_logp) * (policy_logp - ref_logp - kl_raw[:, None])
    ).astype(BF16)
    return (grad_policy, stats[5] - ref_lse, live * kl_raw)


def solution(mesh):
    fine = Mesh(mesh.devices.reshape(NX, NZ, NY, NC), VOC)
    in_specs = (
        P(PIPE, TP),
        P(None, PIPE),
        P(TP, PIPE),
        P(PIPE),
        P(None, VOC),
        P(VOC),
        P(None, VOC),
        P(),
        P(),
        P(),
    )
    out_specs = (P(None, VOC), P(), P())
    return jax.shard_map(
        on_device, mesh=fine, in_specs=in_specs, out_specs=out_specs, check_vma=False
    )
```

```python
import jax
import jax.numpy as jnp
from jax import lax
from jax.sharding import Mesh, PartitionSpec as P

D = 8192
RESP = 64
NX, NZ, NY, NC = 4, 16, 4, 2
PIPE = ("x", "z")
TP = ("y", "c")
VOC = ("x", "z", "y", "c")
BF16, F32 = jnp.bfloat16, jnp.float32


def share(block, axes, count):
    return lax.all_to_all(jnp.broadcast_to(block[None], (count,) + block.shape), axes, 0, 0)


def pieces(value):
    high = lax.reduce_precision(value, 8, 7)
    mid = lax.reduce_precision(value - high, 8, 7)
    low = value - high - mid
    return high.astype(BF16), mid.astype(BF16), low.astype(BF16)


def join(high, mid, low):
    return high.astype(F32) + mid.astype(F32) + low.astype(F32)


def swap_cores(value):
    return lax.ppermute(value, "c", [(0, 1), (1, 0)])


def combine(stats):
    ref, policy, kl, picked = (stats[:, i] for i in range(4))
    ref_top, policy_top = jnp.max(ref, axis=0), jnp.max(policy, axis=0)
    ref_lse = ref_top + jnp.log(jnp.sum(jnp.exp(ref - ref_top), axis=0))
    policy_lse = policy_top + jnp.log(jnp.sum(jnp.exp(policy - policy_top), axis=0))
    policy_part = policy - policy_lse
    kl = jnp.sum(jnp.exp(policy_part) * (kl + policy_part - (ref - ref_lse)), axis=0)
    return jnp.stack([ref_lse, policy_lse, kl, jnp.sum(picked, axis=0)])


def device(x, z, y, c):
    return ((x * NZ + z) * NY + y) * NC + c


def along_x(c):
    return [[device(x, z, y, c) for x in range(NX)] for z in range(NZ) for y in range(NY)]


def along_y(c):
    return [[device(x, z, y, c) for y in range(NY)] for z in range(NZ) for x in range(NX)]


def share_plane(block):
    first, second = along_x(0) + along_y(1), along_y(0) + along_x(1)
    block = jnp.broadcast_to(block[None], (4,) + block.shape)
    block = lax.all_to_all(block, VOC, 0, 0, axis_index_groups=first)
    block = jnp.broadcast_to(block[None], (4,) + block.shape)
    return lax.all_to_all(block, VOC, 0, 0, axis_index_groups=second)


def natural_order(value, c):
    blocks = value.reshape((4, 4, -1) + value.shape[1:])
    return jnp.where(c == 0, blocks.swapaxes(0, 1), blocks).reshape(value.shape)


def on_device(
    attn_out,
    residual,
    o_weight,
    norm_gain,
    head_weight,
    head_scale,
    policy_logits,
    token_ids,
    lengths,
    loss_mask,
):
    y, c = lax.axis_index("y"), lax.axis_index("c")
    tokens = residual.shape[0]
    rows_x = tokens // NX
    rows = rows_x // NY
    cols = o_weight.shape[1]
    depth = o_weight.shape[0]
    half = D // NC
    vocab_dev = head_weight.shape[1]

    attn = share(attn_out, "z", NZ).reshape(rows_x, depth)
    gain_rows = jnp.concatenate(
        [jnp.stack(pieces(norm_gain)), jnp.zeros((13, cols), BF16)]
    )
    to_x = jnp.concatenate(
        [
            jnp.broadcast_to(o_weight[None], (NX, depth, cols)),
            residual.reshape(NX, rows_x, cols),
            jnp.broadcast_to(gain_rows[None], (NX, 16, cols)),
        ],
        axis=1,
    )
    from_x = lax.all_to_all(to_x, "x", 0, 0)
    terms = jnp.stack(
        [
            jnp.dot(attn, from_x[i, :depth], preferred_element_type=F32)
            for i in range(NX)
        ]
    )
    terms = terms.reshape(NC, NX // NC, NY, rows, cols).transpose(2, 0, 1, 3, 4)
    terms, head_weight = lax.optimization_barrier((terms, head_weight))
    own_weight = lax.dynamic_slice_in_dim(head_weight, c * half, half, 0)
    peer_weight = swap_cores(lax.dynamic_slice_in_dim(head_weight, (1 - c) * half, half, 0))
    terms = lax.all_to_all(terms.reshape(NY * NC, NX // NC, rows, cols), TP, 0, 0)
    own_from = lax.dynamic_slice_in_dim(from_x, c * (NX // NC), NX // NC, 0)
    own_residual = lax.dynamic_slice_in_dim(
        own_from[:, depth : depth + rows_x], y * rows, rows, 1
    )
    gain = join(*(own_from[:, depth + rows_x + i] for i in range(3)))
    stream = own_residual.astype(F32) + jnp.sum(terms, axis=0)
    squares = jnp.sum(stream * stream, axis=(0, 2))
    scaled = (stream * gain[:, None, :]).astype(BF16)

    square_rows = jnp.concatenate(
        [jnp.concatenate(pieces(squares)), jnp.zeros((cols - 3 * rows,), BF16)]
    )
    to_z = jnp.concatenate(
        [
            scaled.reshape(NX // NC * rows, cols),
            jnp.broadcast_to(square_rows[None], (16, cols)),
        ]
    )
    from_z = share(to_z, "z", NZ)
    features = from_z[:, : NX // NC * rows].reshape(NZ, NX // NC, rows, cols)
    features = features.transpose(2, 1, 0, 3).reshape(rows, half)
    square_z = from_z[:, NX // NC * rows]
    squares = jnp.sum(
        join(*(square_z[:, i * rows : (i + 1) * rows] for i in range(3))), axis=0
    )
    square_cols = jnp.concatenate(
        [jnp.stack(pieces(squares), axis=1), jnp.zeros((rows, 125), BF16)], axis=1
    )
    to_plane, peer_weight = lax.optimization_barrier(
        (jnp.concatenate([features, square_cols], axis=1), peer_weight)
    )
    hidden = share_plane(to_plane).reshape(tokens, half + 128)
    squares = natural_order(join(*(hidden[:, half + i] for i in range(3))), c)
    squares = squares + swap_cores(squares)
    hidden = hidden[:, :half]
    peer_logits = jnp.dot(hidden, peer_weight, preferred_element_type=F32)
    peer_logits = swap_cores(natural_order(peer_logits, c))
    raw_logits = jnp.dot(hidden, own_weight, preferred_element_type=F32)
    raw_logits = natural_order(raw_logits, c) + peer_logits
    row_scale = lax.rsqrt(squares / D + 1e-06)
    ref_logits = raw_logits * row_scale[:, None] * head_scale[None, :]

    policy = policy_logits.astype(F32)
    columns = lax.axis_index(VOC) * vocab_dev + jnp.arange(vocab_dev, dtype=jnp.int32)
    picked = jnp.sum(
        jnp.where(token_ids[:, None] == columns[None, :], ref_logits, 0.0), axis=1
    )
    ref_max, policy_max = jnp.max(ref_logits, axis=1), jnp.max(policy, axis=1)
    ref_down = ref_logits - ref_max[:, None]
    policy_down = policy - policy_max[:, None]
    policy_exp = jnp.exp(policy_down)
    ref_sum, policy_sum = jnp.sum(jnp.exp(ref_down), axis=1), jnp.sum(policy_exp, axis=1)
    ref_log, policy_log = jnp.log(ref_sum), jnp.log(policy_sum)
    kl_part = jnp.sum(policy_exp * (policy_down - ref_down), axis=1) / policy_sum
    kl_part = kl_part - policy_log + ref_log
    positions = jnp.arange(tokens, dtype=jnp.int32)
    slots = jnp.arange(lengths.shape[0], dtype=jnp.int32)
    seq_len = jnp.sum(
        jnp.where((positions // RESP)[:, None] == slots[None, :], lengths[None, :], 0), axis=1
    )
    live = jnp.where((positions % RESP < seq_len) & (loss_mask > 0), 1.0, 0.0).astype(F32)
    stats = jnp.stack([ref_max + ref_log, policy_max + policy_log, kl_part, picked])
    stats, live = lax.optimization_barrier((stats, live))
    stats = combine(share(stats, ("x", "y", "c"), NX * NY * NC))
    ref_lse, policy_lse, kl_raw, picked = combine(share(stats, "z", NZ))
    ref_logp = ref_logits - ref_lse[:, None]
    policy_logp = policy - policy_lse[:, None]
    grad_policy = (
        live[:, None] * jnp.exp(policy_logp) * (policy_logp - ref_logp - kl_raw[:, None])
    ).astype(BF16)
    return (grad_policy, picked - ref_lse, live * kl_raw)


def solution(mesh):
    fine = Mesh(mesh.devices.reshape(NX, NZ, NY, NC), VOC)
    in_specs = (
        P(PIPE, TP),
        P(None, PIPE),
        P(TP, PIPE),
        P(PIPE),
        P(None, VOC),
        P(VOC),
        P(None, VOC),
        P(),
        P(),
        P(),
    )
    out_specs = (P(None, VOC), P(), P())
    return jax.shard_map(
        on_device, mesh=fine, in_specs=in_specs, out_specs=out_specs, check_vma=False
    )
```

```python
import jax
import jax.numpy as jnp
from jax import lax
from jax.sharding import Mesh, PartitionSpec as P

D = 8192
RESP = 64
NX, NZ, NY, NC = 4, 16, 4, 2
PIPE = ("x", "z")
TP = ("y", "c")
VOC = ("x", "z", "y", "c")
BF16, F32 = jnp.bfloat16, jnp.float32


def share(block, axes, count):
    return lax.all_to_all(jnp.broadcast_to(block[None], (count,) + block.shape), axes, 0, 0)


def pieces(value):
    high = lax.reduce_precision(value, 8, 7)
    mid = lax.reduce_precision(value - high, 8, 7)
    low = value - high - mid
    return high.astype(BF16), mid.astype(BF16), low.astype(BF16)


def join(high, mid, low):
    return high.astype(F32) + mid.astype(F32) + low.astype(F32)


def swap_cores(value):
    return lax.ppermute(value, "c", [(0, 1), (1, 0)])


def combine(stats):
    ref, policy, kl, picked = (stats[:, i] for i in range(4))
    ref_top, policy_top = jnp.max(ref, axis=0), jnp.max(policy, axis=0)
    ref_lse = ref_top + jnp.log(jnp.sum(jnp.exp(ref - ref_top), axis=0))
    policy_lse = policy_top + jnp.log(jnp.sum(jnp.exp(policy - policy_top), axis=0))
    policy_part = policy - policy_lse
    kl = jnp.sum(jnp.exp(policy_part) * (kl + policy_part - (ref - ref_lse)), axis=0)
    return jnp.stack([ref_lse, policy_lse, kl, jnp.sum(picked, axis=0)])


def device(x, z, y, c):
    return ((x * NZ + z) * NY + y) * NC + c


def along_x(c):
    return [[device(x, z, y, c) for x in range(NX)] for z in range(NZ) for y in range(NY)]


def along_y(c):
    return [[device(x, z, y, c) for y in range(NY)] for z in range(NZ) for x in range(NX)]


FIRST, SECOND = along_x(0) + along_y(1), along_y(0) + along_x(1)


def shift_second(value, by):
    pairs = [(g[i], g[(i + by) % 4]) for g in SECOND for i in range(4)]
    return lax.ppermute(value, VOC, pairs)


def on_device(
    attn_out,
    residual,
    o_weight,
    norm_gain,
    head_weight,
    head_scale,
    policy_logits,
    token_ids,
    lengths,
    loss_mask,
):
    tokens = residual.shape[0]
    rows_x = tokens // NX
    rows = rows_x // NY
    cols = o_weight.shape[1]
    depth = o_weight.shape[0]
    half = D // NC
    vocab_dev = head_weight.shape[1]

    gain_rows = jnp.concatenate(
        [jnp.stack(pieces(norm_gain)), jnp.zeros((13, cols), BF16)]
    )
    to_x = jnp.concatenate(
        [
            jnp.broadcast_to(o_weight[None], (NX, depth, cols)),
            residual.reshape(NX, rows_x, cols),
            jnp.broadcast_to(gain_rows[None], (NX, 16, cols)),
        ],
        axis=1,
    )
    from_x = lax.all_to_all(to_x, "x", 0, 0)
    attn_out, from_x = lax.optimization_barrier((attn_out, from_x))
    attn = share(attn_out, "z", NZ).reshape(rows_x, depth)
    attn, from_x, me = lax.optimization_barrier((attn, from_x, lax.axis_index(VOC)))
    c, y, x = me & 1, (me >> 1) & 3, me >> 7
    terms = jnp.stack(
        [
            jnp.dot(attn, from_x[i, :depth], preferred_element_type=F32)
            for i in range(NX)
        ]
    )
    terms = terms.reshape(NC, NX // NC, NY, rows, cols).transpose(2, 0, 1, 3, 4)
    terms, head_weight = lax.optimization_barrier((terms, head_weight))
    peer_weight = swap_cores(lax.dynamic_slice_in_dim(head_weight, (1 - c) * half, half, 0))
    terms = lax.all_to_all(terms.reshape(NY * NC, NX // NC, rows, cols), TP, 0, 0)
    own_from = lax.dynamic_slice_in_dim(from_x, c * (NX // NC), NX // NC, 0)
    own_residual = lax.dynamic_slice_in_dim(
        own_from[:, depth : depth + rows_x], y * rows, rows, 1
    )
    gain = join(*(own_from[:, depth + rows_x + i] for i in range(3)))
    stream = own_residual.astype(F32) + jnp.sum(terms, axis=0)
    squares = jnp.sum(stream * stream, axis=(0, 2))
    scaled = (stream * gain[:, None, :]).astype(BF16)

    square_rows = jnp.concatenate(
        [jnp.concatenate(pieces(squares)), jnp.zeros((cols - 3 * rows,), BF16)]
    )
    to_z = jnp.concatenate(
        [
            scaled.reshape(NX // NC * rows, cols),
            jnp.broadcast_to(square_rows[None], (16, cols)),
        ]
    )
    from_z = share(to_z, "z", NZ)
    features = from_z[:, : NX // NC * rows].reshape(NZ, NX // NC, rows, cols)
    features = features.transpose(2, 1, 0, 3).reshape(rows, half)
    square_z = from_z[:, NX // NC * rows]
    squares = jnp.sum(
        join(*(square_z[:, i * rows : (i + 1) * rows] for i in range(3))), axis=0
    )
    square_cols = jnp.concatenate(
        [jnp.stack(pieces(squares), axis=1), jnp.zeros((rows, 125), BF16)], axis=1
    )
    block, peer_weight = lax.optimization_barrier(
        (jnp.concatenate([features, square_cols], axis=1), peer_weight)
    )
    block = lax.all_to_all(
        jnp.broadcast_to(block[None], (4,) + block.shape), VOC, 0, 0, axis_index_groups=FIRST
    ).reshape(rows_x, half + 128)
    block, head_weight, policy_logits, token_ids, lengths, loss_mask, head_scale = (
        lax.optimization_barrier(
            (block, head_weight, policy_logits, token_ids, lengths, loss_mask, head_scale)
        )
    )
    own_weight = lax.optimization_barrier(
        lax.dynamic_slice_in_dim(head_weight, c * half, half, 0)
    )
    blocks = [(0, block)] + [(by, shift_second(block, by)) for by in (2, 1, 3)]
    place = jnp.where(c == 0, y, x)
    own_logits = jnp.zeros((4, rows_x, vocab_dev), F32)
    own_squares = jnp.zeros((4, 1, rows_x), F32)
    for_peer = jnp.zeros((4, rows_x + 8, vocab_dev), F32)
    for by, block in blocks:
        at = (place - by) & 3
        hidden = block[:, :half]
        part = join(*(block[:, half + i] for i in range(3)))[None, None]
        own_part = jnp.dot(hidden, own_weight, preferred_element_type=F32)[None]
        peer_part = jnp.dot(hidden, peer_weight, preferred_element_type=F32)[None]
        own_squares = lax.dynamic_update_slice(own_squares, part, (at, 0, 0))
        own_logits = lax.dynamic_update_slice(own_logits, own_part, (at, 0, 0))
        for_peer = lax.dynamic_update_slice(for_peer, part, (at, rows_x, 0))
        for_peer = lax.dynamic_update_slice(for_peer, peer_part, (at, 0, 0))
    from_peer = swap_cores(for_peer)

    def both(own, peer):
        shape = (4, 4, rows) + own.shape[2:]
        own, peer = own.reshape(shape), peer.reshape(shape)
        first = jnp.where(c == 0, own, peer).swapaxes(0, 1)
        return (first + jnp.where(c == 0, peer, own)).reshape((tokens,) + shape[3:])

    squares = both(own_squares[:, 0], from_peer[:, rows_x, :rows_x])
    raw_logits = both(own_logits, from_peer[:, :rows_x])
    row_scale = lax.rsqrt(squares / D + 1e-06)
    ref_logits = raw_logits * row_scale[:, None] * head_scale[None, :]

    policy = policy_logits.astype(F32)
    columns = me * vocab_dev + jnp.arange(vocab_dev, dtype=jnp.int32)
    picked = jnp.sum(
        jnp.where(token_ids[:, None] == columns[None, :], ref_logits, 0.0), axis=1
    )
    ref_max, policy_max = jnp.max(ref_logits, axis=1), jnp.max(policy, axis=1)
    ref_down = ref_logits - ref_max[:, None]
    policy_down = policy - policy_max[:, None]
    policy_exp = jnp.exp(policy_down)
    ref_sum, policy_sum = jnp.sum(jnp.exp(ref_down), axis=1), jnp.sum(policy_exp, axis=1)
    ref_log, policy_log = jnp.log(ref_sum), jnp.log(policy_sum)
    kl_part = jnp.sum(policy_exp * (policy_down - ref_down), axis=1) / policy_sum
    kl_part = kl_part - policy_log + ref_log
    positions = jnp.arange(tokens, dtype=jnp.int32)
    slots = jnp.arange(lengths.shape[0], dtype=jnp.int32)
    seq_len = jnp.sum(
        jnp.where((positions // RESP)[:, None] == slots[None, :], lengths[None, :], 0), axis=1
    )
    live = jnp.where((positions % RESP < seq_len) & (loss_mask > 0), 1.0, 0.0).astype(F32)
    stats = jnp.stack([ref_max + ref_log, policy_max + policy_log, kl_part, picked])
    stats, live = lax.optimization_barrier((stats, live))
    stats = combine(share(stats, ("x", "y", "c"), NX * NY * NC))
    ref_lse, policy_lse, kl_raw, picked = combine(share(stats, "z", NZ))
    ref_logp = ref_logits - ref_lse[:, None]
    policy_logp = policy - policy_lse[:, None]
    grad_policy = (
        live[:, None] * jnp.exp(policy_logp) * (policy_logp - ref_logp - kl_raw[:, None])
    ).astype(BF16)
    return (grad_policy, picked - ref_lse, live * kl_raw)


def solution(mesh):
    fine = Mesh(mesh.devices.reshape(NX, NZ, NY, NC), VOC)
    in_specs = (
        P(PIPE, TP),
        P(None, PIPE),
        P(TP, PIPE),
        P(PIPE),
        P(None, VOC),
        P(VOC),
        P(None, VOC),
        P(),
        P(),
        P(),
    )
    out_specs = (P(None, VOC), P(), P())
    return jax.shard_map(
        on_device, mesh=fine, in_specs=in_specs, out_specs=out_specs, check_vma=False
    )
```

```python
import jax
import jax.numpy as jnp
from jax import lax
from jax.sharding import Mesh, PartitionSpec as P

D = 8192
RESP = 64
NX, NZ, NY, NC = 4, 16, 4, 2
PIPE = ("x", "z")
TP = ("y", "c")
VOC = ("x", "z", "y", "c")
BF16, F32 = jnp.bfloat16, jnp.float32


def share(block, axes, count):
    return lax.all_to_all(jnp.broadcast_to(block[None], (count,) + block.shape), axes, 0, 0)


def pieces(value):
    high = lax.reduce_precision(value, 8, 7)
    mid = lax.reduce_precision(value - high, 8, 7)
    low = value - high - mid
    return high.astype(BF16), mid.astype(BF16), low.astype(BF16)


def join(high, mid, low):
    return high.astype(F32) + mid.astype(F32) + low.astype(F32)


def swap_cores(value):
    return lax.ppermute(value, "c", [(0, 1), (1, 0)])


def combine(stats):
    ref, policy, kl, picked = (stats[:, i] for i in range(4))
    ref_top, policy_top = jnp.max(ref, axis=0), jnp.max(policy, axis=0)
    ref_lse = ref_top + jnp.log(jnp.sum(jnp.exp(ref - ref_top), axis=0))
    policy_lse = policy_top + jnp.log(jnp.sum(jnp.exp(policy - policy_top), axis=0))
    policy_part = policy - policy_lse
    kl = jnp.sum(jnp.exp(policy_part) * (kl + policy_part - (ref - ref_lse)), axis=0)
    return jnp.stack([ref_lse, policy_lse, kl, jnp.sum(picked, axis=0)])


def device(x, z, y, c):
    return ((x * NZ + z) * NY + y) * NC + c


def along_x(c):
    return [[device(x, z, y, c) for x in range(NX)] for z in range(NZ) for y in range(NY)]


def along_y(c):
    return [[device(x, z, y, c) for y in range(NY)] for z in range(NZ) for x in range(NX)]


def share_plane(block):
    first, second = along_x(0) + along_y(1), along_y(0) + along_x(1)
    block = jnp.broadcast_to(block[None], (4,) + block.shape)
    block = lax.all_to_all(block, VOC, 0, 0, axis_index_groups=first)
    block = jnp.broadcast_to(block[None], (4,) + block.shape)
    return lax.all_to_all(block, VOC, 0, 0, axis_index_groups=second)


def natural_order(value, c):
    blocks = value.reshape((4, 4, -1) + value.shape[1:])
    return jnp.where(c == 0, blocks.swapaxes(0, 1), blocks).reshape(value.shape)


def on_device(
    attn_out,
    residual,
    o_weight,
    norm_gain,
    head_weight,
    head_scale,
    policy_logits,
    token_ids,
    lengths,
    loss_mask,
):
    tokens = residual.shape[0]
    rows_x = tokens // NX
    rows = rows_x // NY
    cols = o_weight.shape[1]
    depth = o_weight.shape[0]
    half = D // NC
    vocab_dev = head_weight.shape[1]

    gain_rows = jnp.concatenate(
        [jnp.stack(pieces(norm_gain)), jnp.zeros((13, cols), BF16)]
    )
    to_x = jnp.concatenate(
        [
            jnp.broadcast_to(o_weight[None], (NX, depth, cols)),
            residual.reshape(NX, rows_x, cols),
            jnp.broadcast_to(gain_rows[None], (NX, 16, cols)),
        ],
        axis=1,
    )
    positions = jnp.arange(tokens, dtype=jnp.int32)
    to_x, me, positions = lax.optimization_barrier((to_x, lax.axis_index(VOC), positions))
    from_x = lax.all_to_all(to_x, "x", 0, 0)
    attn_out, from_x, me = lax.optimization_barrier((attn_out, from_x, me))
    attn = share(attn_out, "z", NZ).reshape(rows_x, depth)
    attn, from_x, me = lax.optimization_barrier((attn, from_x, me))
    c, y = me & 1, (me >> 1) & 3
    all_residual, all_gain = lax.optimization_barrier(
        (
            from_x[:, depth : depth + rows_x],
            join(*(from_x[:, depth + rows_x + i] for i in range(3))),
        )
    )
    terms = jnp.stack(
        [
            jnp.dot(attn, from_x[i, :depth], preferred_element_type=F32)
            for i in range(NX)
        ]
    )
    terms = terms.reshape(NC, NX // NC, NY, rows, cols).transpose(2, 0, 1, 3, 4)
    inputs = (head_weight, policy_logits, token_ids, lengths, loss_mask, positions)
    terms, inputs = lax.optimization_barrier((terms, inputs))
    head_weight, policy_logits, token_ids, lengths, loss_mask, positions = inputs
    peer_weight = swap_cores(lax.dynamic_slice_in_dim(head_weight, (1 - c) * half, half, 0))
    policy_max = jnp.max(policy_logits, axis=1).astype(F32)
    policy_sum = jnp.sum(jnp.exp(policy_logits.astype(F32) - policy_max[:, None]), axis=1)
    policy_log = jnp.log(policy_sum)
    slots = jnp.arange(lengths.shape[0], dtype=jnp.int32)
    seq_len = jnp.sum(
        jnp.where((positions // RESP)[:, None] == slots[None, :], lengths[None, :], 0), axis=1
    )
    live = jnp.where((positions % RESP < seq_len) & (loss_mask > 0), 1.0, 0.0).astype(F32)
    own_residual = lax.dynamic_slice(
        all_residual, (c * (NX // NC), y * rows, 0), (NX // NC, rows, cols)
    )
    gain = lax.dynamic_slice_in_dim(all_gain, c * (NX // NC), NX // NC, 0)
    terms = lax.all_to_all(terms.reshape(NY * NC, NX // NC, rows, cols), TP, 0, 0)
    terms, own_residual, gain, me, policy_max, policy_sum, policy_log, live = (
        lax.optimization_barrier(
            (terms, own_residual, gain, me, policy_max, policy_sum, policy_log, live)
        )
    )
    stream = own_residual.astype(F32) + jnp.sum(terms, axis=0)
    squares = jnp.sum(stream * stream, axis=(0, 2))
    scaled = stream * gain[:, None, :]

    square_row = jnp.concatenate([squares, jnp.zeros((cols - rows,), F32)])
    to_z = jnp.concatenate(
        [
            scaled.reshape(NX // NC * rows, cols),
            jnp.broadcast_to(square_row[None], (8, cols)),
        ]
    )
    to_z, peer_weight = lax.optimization_barrier((to_z, peer_weight))
    from_z = share(to_z, "z", NZ)
    squares = jnp.sum(from_z[:, NX // NC * rows, :rows], axis=0)
    squares = squares + swap_cores(squares)
    row_scale = lax.rsqrt(squares / D + 1e-06)
    features = from_z[:, : NX // NC * rows].reshape(NZ, NX // NC, rows, cols)
    features = (features * row_scale[:, None]).astype(BF16)
    features = features.transpose(2, 1, 0, 3).reshape(rows, half)
    hidden = share_plane(features).reshape(tokens, half)
    hidden, me = lax.optimization_barrier((hidden, me))
    c = me & 1
    own_weight = lax.dynamic_slice_in_dim(head_weight, c * half, half, 0)
    peer_logits = jnp.dot(hidden, peer_weight, preferred_element_type=F32)
    peer_logits = swap_cores(natural_order(peer_logits, c))
    raw_logits = jnp.dot(hidden, own_weight, preferred_element_type=F32)
    raw_logits = natural_order(raw_logits, c) + peer_logits
    ref_logits = raw_logits * head_scale[None, :]

    policy = policy_logits.astype(F32)
    columns = me * vocab_dev + jnp.arange(vocab_dev, dtype=jnp.int32)
    picked = jnp.sum(
        jnp.where(token_ids[:, None] == columns[None, :], ref_logits, 0.0), axis=1
    )
    ref_max = jnp.max(ref_logits, axis=1)
    ref_down = ref_logits - ref_max[:, None]
    policy_down = policy - policy_max[:, None]
    policy_exp = jnp.exp(policy_down)
    ref_log = jnp.log(jnp.sum(jnp.exp(ref_down), axis=1))
    kl_part = jnp.sum(policy_exp * (policy_down - ref_down), axis=1) / policy_sum
    kl_part = kl_part - policy_log + ref_log
    stats = jnp.stack([ref_max + ref_log, policy_max + policy_log, kl_part, picked])
    stats = combine(share(stats, ("x", "y", "c"), NX * NY * NC))
    ref_lse, policy_lse, kl_raw, picked = combine(share(stats, "z", NZ))
    ref_logp = ref_logits - ref_lse[:, None]
    policy_logp = policy - policy_lse[:, None]
    grad_policy = (
        live[:, None] * jnp.exp(policy_logp) * (policy_logp - ref_logp - kl_raw[:, None])
    ).astype(BF16)
    return (grad_policy, picked - ref_lse, live * kl_raw)


def solution(mesh):
    fine = Mesh(mesh.devices.reshape(NX, NZ, NY, NC), VOC)
    in_specs = (
        P(PIPE, TP),
        P(None, PIPE),
        P(TP, PIPE),
        P(PIPE),
        P(None, VOC),
        P(VOC),
        P(None, VOC),
        P(),
        P(),
        P(),
    )
    out_specs = (P(None, VOC), P(), P())
    return jax.shard_map(
        on_device, mesh=fine, in_specs=in_specs, out_specs=out_specs, check_vma=False
    )
```

```python
import jax
import jax.numpy as jnp
from jax import lax
from jax.experimental import pallas as pl
from jax.experimental.pallas import tpu as pltpu
from jax.sharding import Mesh, PartitionSpec as P

D = 8192
RESP = 64
NX, NZ, NY, NC = 4, 16, 4, 2
PIPE = ("x", "z")
TP = ("y", "c")
VOC = ("x", "z", "y", "c")
BF16, F32 = jnp.bfloat16, jnp.float32


def share(block, axes, count):
    return lax.all_to_all(jnp.broadcast_to(block[None], (count,) + block.shape), axes, 0, 0)


def pieces(value):
    high = lax.reduce_precision(value, 8, 7)
    mid = lax.reduce_precision(value - high, 8, 7)
    low = value - high - mid
    return high.astype(BF16), mid.astype(BF16), low.astype(BF16)


def join(high, mid, low):
    return high.astype(F32) + mid.astype(F32) + low.astype(F32)


def swap_cores(value):
    return lax.ppermute(value, "c", [(0, 1), (1, 0)])


def combine(stats):
    ref, policy, kl, picked = (stats[:, i] for i in range(4))
    ref_top, policy_top = jnp.max(ref, axis=0), jnp.max(policy, axis=0)
    ref_lse = ref_top + jnp.log(jnp.sum(jnp.exp(ref - ref_top), axis=0))
    policy_lse = policy_top + jnp.log(jnp.sum(jnp.exp(policy - policy_top), axis=0))
    policy_part = policy - policy_lse
    kl = jnp.sum(jnp.exp(policy_part) * (kl + policy_part - (ref - ref_lse)), axis=0)
    return jnp.stack([ref_lse, policy_lse, kl, jnp.sum(picked, axis=0)])


def device(x, z, y, c):
    return ((x * NZ + z) * NY + y) * NC + c


def along_x(c):
    return [[device(x, z, y, c) for x in range(NX)] for z in range(NZ) for y in range(NY)]


def along_y(c):
    return [[device(x, z, y, c) for y in range(NY)] for z in range(NZ) for x in range(NX)]


def share_plane(block):
    first, second = along_x(0) + along_y(1), along_y(0) + along_x(1)
    block = jnp.broadcast_to(block[None], (4,) + block.shape)
    block = lax.all_to_all(block, VOC, 0, 0, axis_index_groups=first)
    block = jnp.broadcast_to(block[None], (4,) + block.shape)
    return lax.all_to_all(block, VOC, 0, 0, axis_index_groups=second)


def head_kernel(core, hidden, own_weight, peer_weight, own_out, peer_out, own_sum, peer_sum):
    step = pl.program_id(0)
    block = hidden[...].reshape(own_sum.shape[0], hidden.shape[-1])
    own = jnp.dot(block, own_weight[...], preferred_element_type=F32)
    peer = jnp.dot(block, peer_weight[...], preferred_element_type=F32)

    @pl.when(step == 0)
    def _():
        own_sum[...] = own
        peer_sum[...] = peer

    @pl.when(step > 0)
    def _():
        own_sum[...] += own
        peer_sum[...] += peer

    @pl.when(step == pl.num_programs(0) - 1)
    def _():
        rows = hidden.shape[2]
        for i in range(4):
            for j in range(4):
                to = jnp.where(core[0] == 0, j * 4 + i, i * 4 + j)
                at = pl.ds(pl.multiple_of(to * rows, rows), rows)
                own_out[at, :] = own_sum[pl.ds((i * 4 + j) * rows, rows), :]
                peer_out[at, :] = peer_sum[pl.ds((i * 4 + j) * rows, rows), :]


def head(core, hidden, own_weight, peer_weight):
    depth = 512
    steps = hidden.shape[-1] // depth
    tokens, cols = 16 * hidden.shape[2], own_weight.shape[1]
    weight = pl.BlockSpec((depth, cols), lambda k, core: (core[0] * steps + k, 0))
    out = pl.BlockSpec((tokens, cols), lambda k, core: (0, 0))
    return pl.pallas_call(
        head_kernel,
        grid_spec=pltpu.PrefetchScalarGridSpec(
            num_scalar_prefetch=1,
            grid=(steps,),
            in_specs=[
                pl.BlockSpec(hidden.shape[:3] + (depth,), lambda k, core: (0, 0, 0, k)),
                weight,
                weight,
            ],
            out_specs=[out, out],
            scratch_shapes=[pltpu.VMEM((tokens, cols), F32)] * 2,
        ),
        out_shape=[jax.ShapeDtypeStruct((tokens, cols), F32)] * 2,
        compiler_params=pltpu.CompilerParams(vmem_limit_bytes=60 * 2**20),
        cost_estimate=pl.CostEstimate(
            flops=4 * tokens * cols * hidden.shape[-1],
            bytes_accessed=2 * hidden.size + 4 * hidden.shape[-1] * cols,
            transcendentals=0,
        ),
    )(core.reshape(1).astype(jnp.int32), hidden, own_weight, peer_weight)


def on_device(
    attn_out,
    residual,
    o_weight,
    norm_gain,
    head_weight,
    head_scale,
    policy_logits,
    token_ids,
    lengths,
    loss_mask,
):
    tokens = residual.shape[0]
    rows_x = tokens // NX
    rows = rows_x // NY
    cols = o_weight.shape[1]
    depth = o_weight.shape[0]
    half = D // NC
    vocab_dev = head_weight.shape[1]

    gain_rows = jnp.concatenate(
        [jnp.stack(pieces(norm_gain)), jnp.zeros((13, cols), BF16)]
    )
    to_x = jnp.concatenate(
        [
            jnp.broadcast_to(o_weight[None], (NX, depth, cols)),
            residual.reshape(NX, rows_x, cols),
            jnp.broadcast_to(gain_rows[None], (NX, 16, cols)),
        ],
        axis=1,
    )
    positions = jnp.arange(tokens, dtype=jnp.int32)
    to_x, me, positions = lax.optimization_barrier((to_x, lax.axis_index(VOC), positions))
    from_x = lax.all_to_all(to_x, "x", 0, 0)
    attn_out, from_x, me, head_weight = lax.optimization_barrier(
        (attn_out, from_x, me, head_weight)
    )
    peer_weight = swap_cores(head_weight)
    attn = share(attn_out, "z", NZ).reshape(rows_x, depth)
    attn, from_x, me = lax.optimization_barrier((attn, from_x, me))
    c, y = me & 1, (me >> 1) & 3
    all_residual, all_gain = lax.optimization_barrier(
        (
            from_x[:, depth : depth + rows_x],
            join(*(from_x[:, depth + rows_x + i] for i in range(3))),
        )
    )
    terms = jnp.stack(
        [
            jnp.dot(attn, from_x[i, :depth], preferred_element_type=F32)
            for i in range(NX)
        ]
    )
    terms = terms.reshape(NC, NX // NC, NY, rows, cols).transpose(2, 0, 1, 3, 4)
    inputs = (policy_logits, token_ids, lengths, loss_mask, positions)
    terms, inputs = lax.optimization_barrier((terms, inputs))
    policy_logits, token_ids, lengths, loss_mask, positions = inputs
    policy_max = jnp.max(policy_logits, axis=1).astype(F32)
    policy_sum = jnp.sum(jnp.exp(policy_logits.astype(F32) - policy_max[:, None]), axis=1)
    policy_log = jnp.log(policy_sum)
    slots = jnp.arange(lengths.shape[0], dtype=jnp.int32)
    seq_len = jnp.sum(
        jnp.where((positions // RESP)[:, None] == slots[None, :], lengths[None, :], 0), axis=1
    )
    live = jnp.where((positions % RESP < seq_len) & (loss_mask > 0), 1.0, 0.0).astype(F32)
    own_residual = lax.dynamic_slice(
        all_residual, (c * (NX // NC), y * rows, 0), (NX // NC, rows, cols)
    )
    gain = lax.dynamic_slice_in_dim(all_gain, c * (NX // NC), NX // NC, 0)
    terms = lax.all_to_all(terms.reshape(NY * NC, NX // NC, rows, cols), TP, 0, 0)
    terms, own_residual, gain, me, policy_max, policy_sum, policy_log, live, peer_weight = (
        lax.optimization_barrier(
            (terms, own_residual, gain, me, policy_max, policy_sum, policy_log, live, peer_weight)
        )
    )
    stream = own_residual.astype(F32) + jnp.sum(terms, axis=0)
    squares = jnp.sum(stream * stream, axis=(0, 2))
    squares = share(squares[None], ("z", "c"), NZ * NC)
    row_scale = lax.rsqrt(jnp.sum(squares, axis=(0, 1)) / D + 1e-06)
    scaled = (stream * row_scale[:, None] * gain[:, None, :]).astype(BF16)

    to_z = lax.optimization_barrier(scaled.reshape(NX // NC * rows, cols))
    from_z = share(to_z, "z", NZ).reshape(NZ, NX // NC, rows, cols)
    features = from_z.transpose(2, 1, 0, 3).reshape(rows, half)
    hidden, me = lax.optimization_barrier((share_plane(features), me))
    own_logits, peer_logits = head(me & 1, hidden, head_weight, peer_weight)
    raw_logits = own_logits + swap_cores(peer_logits)
    ref_logits = raw_logits * head_scale[None, :]

    policy = policy_logits.astype(F32)
    columns = me * vocab_dev + jnp.arange(vocab_dev, dtype=jnp.int32)
    picked = jnp.sum(
        jnp.where(token_ids[:, None] == columns[None, :], ref_logits, 0.0), axis=1
    )
    ref_max = jnp.max(ref_logits, axis=1)
    ref_down = ref_logits - ref_max[:, None]
    policy_down = policy - policy_max[:, None]
    policy_exp = jnp.exp(policy_down)
    ref_log = jnp.log(jnp.sum(jnp.exp(ref_down), axis=1))
    kl_part = jnp.sum(policy_exp * (policy_down - ref_down), axis=1) / policy_sum
    kl_part = kl_part - policy_log + ref_log
    stats = jnp.stack([ref_max + ref_log, policy_max + policy_log, kl_part, picked])
    stats = combine(share(stats, ("x", "y", "c"), NX * NY * NC))
    ref_lse, policy_lse, kl_raw, picked = combine(share(stats, "z", NZ))
    ref_logp = ref_logits - ref_lse[:, None]
    policy_logp = policy - policy_lse[:, None]
    grad_policy = (
        live[:, None] * jnp.exp(policy_logp) * (policy_logp - ref_logp - kl_raw[:, None])
    ).astype(BF16)
    return (grad_policy, picked - ref_lse, live * kl_raw)


def solution(mesh):
    fine = Mesh(mesh.devices.reshape(NX, NZ, NY, NC), VOC)
    in_specs = (
        P(PIPE, TP),
        P(None, PIPE),
        P(TP, PIPE),
        P(PIPE),
        P(None, VOC),
        P(VOC),
        P(None, VOC),
        P(),
        P(),
        P(),
    )
    out_specs = (P(None, VOC), P(), P())
    return jax.shard_map(
        on_device, mesh=fine, in_specs=in_specs, out_specs=out_specs, check_vma=False
    )
```

```python
import jax
import jax.numpy as jnp
from jax import lax
from jax.experimental import pallas as pl
from jax.experimental.pallas import tpu as pltpu
from jax.sharding import Mesh, PartitionSpec as P

D = 8192
RESP = 64
NX, NZ, NY, NC = 4, 16, 4, 2
PIPE = ("x", "z")
TP = ("y", "c")
VOC = ("x", "z", "y", "c")
BF16, F32 = jnp.bfloat16, jnp.float32


def share(block, axes, count):
    return lax.all_to_all(jnp.broadcast_to(block[None], (count,) + block.shape), axes, 0, 0)


def pieces(value):
    high = lax.reduce_precision(value, 8, 7)
    mid = lax.reduce_precision(value - high, 8, 7)
    low = value - high - mid
    return high.astype(BF16), mid.astype(BF16), low.astype(BF16)


def join(high, mid, low):
    return high.astype(F32) + mid.astype(F32) + low.astype(F32)


def swap_cores(value):
    return lax.ppermute(value, "c", [(0, 1), (1, 0)])


def combine(stats):
    ref, policy, kl, picked = (stats[:, i] for i in range(4))
    ref_top, policy_top = jnp.max(ref, axis=0), jnp.max(policy, axis=0)
    ref_lse = ref_top + jnp.log(jnp.sum(jnp.exp(ref - ref_top), axis=0))
    policy_lse = policy_top + jnp.log(jnp.sum(jnp.exp(policy - policy_top), axis=0))
    policy_part = policy - policy_lse
    kl = jnp.sum(jnp.exp(policy_part) * (kl + policy_part - (ref - ref_lse)), axis=0)
    return jnp.stack([ref_lse, policy_lse, kl, jnp.sum(picked, axis=0)])


def device(x, z, y, c):
    return ((x * NZ + z) * NY + y) * NC + c


def along_x(c):
    return [[device(x, z, y, c) for x in range(NX)] for z in range(NZ) for y in range(NY)]


def along_y(c):
    return [[device(x, z, y, c) for y in range(NY)] for z in range(NZ) for x in range(NX)]


def share_plane(block):
    first, second = along_x(0) + along_y(1), along_y(0) + along_x(1)
    block = jnp.broadcast_to(block[None], (4,) + block.shape)
    block = lax.all_to_all(block, VOC, 0, 0, axis_index_groups=first)
    block = jnp.broadcast_to(block[None], (4,) + block.shape)
    return lax.all_to_all(block, VOC, 0, 0, axis_index_groups=second)


def head_kernel(
    core, hidden, own_weight, peer_weight, own_out, peer_out, held, own_held, peer_held, sums, sems
):
    rows, half = hidden.shape[2:]
    tokens, steps = own_out.shape[0], sems.shape[1]
    depth = half // steps

    def copies(step):
        part = pl.ds(step * depth, depth)
        at = pl.ds(pl.multiple_of(core[0] * half + step * depth, depth), depth)
        return [
            pltpu.make_async_copy(
                hidden.at[:, :, :, part], held.at[:, :, :, part], sems.at[0, step]
            ),
            pltpu.make_async_copy(own_weight.at[at, :], own_held.at[part, :], sems.at[1, step]),
            pltpu.make_async_copy(peer_weight.at[at, :], peer_held.at[part, :], sems.at[2, step]),
        ]

    for step in range(steps):
        for copy in copies(step):
            copy.start()
    for step in range(steps):
        for copy in copies(step):
            copy.wait()
        part = pl.ds(step * depth, depth)
        block = held[:, :, :, part].reshape(tokens, depth)
        for i, weight in enumerate((own_held, peer_held)):
            product = jnp.dot(block, weight[part, :], preferred_element_type=F32)
            sums[i] = product if step == 0 else sums[i] + product
    for i in range(4):
        for j in range(4):
            to = jnp.where(core[0] == 0, j * 4 + i, i * 4 + j)
            at = pl.ds(pl.multiple_of(to * rows, rows), rows)
            own_out[at, :] = sums[0, pl.ds((i * 4 + j) * rows, rows), :]
            peer_out[at, :] = sums[1, pl.ds((i * 4 + j) * rows, rows), :]


def head(core, hidden, own_weight, peer_weight):
    half, steps = hidden.shape[-1], 8
    tokens, cols = 16 * hidden.shape[2], own_weight.shape[1]
    vmem, anywhere = pl.BlockSpec(memory_space=pltpu.VMEM), pl.BlockSpec(memory_space=pl.ANY)
    return pl.pallas_call(
        head_kernel,
        in_specs=[pl.BlockSpec(memory_space=pltpu.SMEM), anywhere, anywhere, anywhere],
        out_specs=[vmem, vmem],
        out_shape=[jax.ShapeDtypeStruct((tokens, cols), F32)] * 2,
        scratch_shapes=[
            pltpu.VMEM(hidden.shape, BF16),
            pltpu.VMEM((half, cols), BF16),
            pltpu.VMEM((half, cols), BF16),
            pltpu.VMEM((2, tokens, cols), F32),
            pltpu.SemaphoreType.DMA((3, steps)),
        ],
        compiler_params=pltpu.CompilerParams(vmem_limit_bytes=60 * 2**20),
        cost_estimate=pl.CostEstimate(
            flops=4 * tokens * cols * half,
            bytes_accessed=2 * hidden.size + 4 * half * cols,
            transcendentals=0,
        ),
    )(core.reshape(1).astype(jnp.int32), hidden, own_weight, peer_weight)


def on_device(
    attn_out,
    residual,
    o_weight,
    norm_gain,
    head_weight,
    head_scale,
    policy_logits,
    token_ids,
    lengths,
    loss_mask,
):
    tokens = residual.shape[0]
    rows_x = tokens // NX
    rows = rows_x // NY
    cols = o_weight.shape[1]
    depth = o_weight.shape[0]
    half = D // NC
    vocab_dev = head_weight.shape[1]

    gain_rows = jnp.concatenate(
        [jnp.stack(pieces(norm_gain)), jnp.zeros((13, cols), BF16)]
    )
    to_x = jnp.concatenate(
        [
            jnp.broadcast_to(o_weight[None], (NX, depth, cols)),
            residual.reshape(NX, rows_x, cols),
            jnp.broadcast_to(gain_rows[None], (NX, 16, cols)),
        ],
        axis=1,
    )
    positions = jnp.arange(tokens, dtype=jnp.int32)
    to_x, me, positions = lax.optimization_barrier((to_x, lax.axis_index(VOC), positions))
    from_x = lax.all_to_all(to_x, "x", 0, 0)
    attn_out, from_x, me, head_weight = lax.optimization_barrier(
        (attn_out, from_x, me, head_weight)
    )
    peer_weight = swap_cores(head_weight)
    attn = share(attn_out, "z", NZ).reshape(rows_x, depth)
    attn, from_x, me = lax.optimization_barrier((attn, from_x, me))
    c, y = me & 1, (me >> 1) & 3
    all_residual, all_gain = lax.optimization_barrier(
        (
            from_x[:, depth : depth + rows_x],
            join(*(from_x[:, depth + rows_x + i] for i in range(3))),
        )
    )
    terms = jnp.stack(
        [
            jnp.dot(attn, from_x[i, :depth], preferred_element_type=F32)
            for i in range(NX)
        ]
    )
    terms = terms.reshape(NC, NX // NC, NY, rows, cols).transpose(2, 0, 1, 3, 4)
    inputs = (policy_logits, token_ids, lengths, loss_mask, positions)
    terms, inputs = lax.optimization_barrier((terms, inputs))
    policy_logits, token_ids, lengths, loss_mask, positions = inputs
    policy_max = jnp.max(policy_logits, axis=1).astype(F32)
    policy_sum = jnp.sum(jnp.exp(policy_logits.astype(F32) - policy_max[:, None]), axis=1)
    policy_log = jnp.log(policy_sum)
    slots = jnp.arange(lengths.shape[0], dtype=jnp.int32)
    seq_len = jnp.sum(
        jnp.where((positions // RESP)[:, None] == slots[None, :], lengths[None, :], 0), axis=1
    )
    live = jnp.where((positions % RESP < seq_len) & (loss_mask > 0), 1.0, 0.0).astype(F32)
    own_residual = lax.dynamic_slice(
        all_residual, (c * (NX // NC), y * rows, 0), (NX // NC, rows, cols)
    )
    gain = lax.dynamic_slice_in_dim(all_gain, c * (NX // NC), NX // NC, 0)
    terms = lax.all_to_all(terms.reshape(NY * NC, NX // NC, rows, cols), TP, 0, 0)
    terms, own_residual, gain, me, policy_max, policy_sum, policy_log, live, peer_weight = (
        lax.optimization_barrier(
            (terms, own_residual, gain, me, policy_max, policy_sum, policy_log, live, peer_weight)
        )
    )
    stream = own_residual.astype(F32) + jnp.sum(terms, axis=0)
    squares = jnp.sum(stream * stream, axis=(0, 2))
    squares = share(squares[None], ("z", "c"), NZ * NC)
    row_scale = lax.rsqrt(jnp.sum(squares, axis=(0, 1)) / D + 1e-06)
    scaled = (stream * row_scale[:, None] * gain[:, None, :]).astype(BF16)

    to_z = lax.optimization_barrier(scaled.reshape(NX // NC * rows, cols))
    from_z = share(to_z, "z", NZ).reshape(NZ, NX // NC, rows, cols)
    features = from_z.transpose(2, 1, 0, 3).reshape(rows, half)
    hidden, me = lax.optimization_barrier((share_plane(features), me))
    own_logits, peer_logits = head(me & 1, hidden, head_weight, peer_weight)
    raw_logits = own_logits + swap_cores(peer_logits)
    ref_logits = raw_logits * head_scale[None, :]

    policy = policy_logits.astype(F32)
    columns = me * vocab_dev + jnp.arange(vocab_dev, dtype=jnp.int32)
    picked = jnp.sum(
        jnp.where(token_ids[:, None] == columns[None, :], ref_logits, 0.0), axis=1
    )
    ref_max = jnp.max(ref_logits, axis=1)
    ref_down = ref_logits - ref_max[:, None]
    policy_down = policy - policy_max[:, None]
    policy_exp = jnp.exp(policy_down)
    ref_log = jnp.log(jnp.sum(jnp.exp(ref_down), axis=1))
    kl_part = jnp.sum(policy_exp * (policy_down - ref_down), axis=1) / policy_sum
    kl_part = kl_part - policy_log + ref_log
    stats = jnp.stack([ref_max + ref_log, policy_max + policy_log, kl_part, picked])
    stats = combine(share(stats, ("x", "y", "c"), NX * NY * NC))
    ref_lse, policy_lse, kl_raw, picked = combine(share(stats, "z", NZ))
    ref_logp = ref_logits - ref_lse[:, None]
    policy_logp = policy - policy_lse[:, None]
    grad_policy = (
        live[:, None] * jnp.exp(policy_logp) * (policy_logp - ref_logp - kl_raw[:, None])
    ).astype(BF16)
    return (grad_policy, picked - ref_lse, live * kl_raw)


def solution(mesh):
    fine = Mesh(mesh.devices.reshape(NX, NZ, NY, NC), VOC)
    in_specs = (
        P(PIPE, TP),
        P(None, PIPE),
        P(TP, PIPE),
        P(PIPE),
        P(None, VOC),
        P(VOC),
        P(None, VOC),
        P(),
        P(),
        P(),
    )
    out_specs = (P(None, VOC), P(), P())
    return jax.shard_map(
        on_device, mesh=fine, in_specs=in_specs, out_specs=out_specs, check_vma=False
    )
```

```python
import jax
import jax.numpy as jnp
from jax import lax
from jax.experimental import pallas as pl
from jax.experimental.pallas import tpu as pltpu
from jax.sharding import Mesh, PartitionSpec as P

D = 8192
RESP = 64
NX, NZ, NY, NC = 4, 16, 4, 2
PIPE = ("x", "z")
TP = ("y", "c")
VOC = ("x", "z", "y", "c")
BF16, F32 = jnp.bfloat16, jnp.float32


def share(block, axes, count):
    return lax.all_to_all(jnp.broadcast_to(block[None], (count,) + block.shape), axes, 0, 0)


def pieces(value):
    high = lax.reduce_precision(value, 8, 7)
    mid = lax.reduce_precision(value - high, 8, 7)
    low = value - high - mid
    return high.astype(BF16), mid.astype(BF16), low.astype(BF16)


def join(high, mid, low):
    return high.astype(F32) + mid.astype(F32) + low.astype(F32)


def swap_cores(value):
    return lax.ppermute(value, "c", [(0, 1), (1, 0)])


def combine(stats):
    ref, policy, kl, picked = (stats[:, i] for i in range(4))
    ref_top, policy_top = jnp.max(ref, axis=0), jnp.max(policy, axis=0)
    ref_lse = ref_top + jnp.log(jnp.sum(jnp.exp(ref - ref_top), axis=0))
    policy_lse = policy_top + jnp.log(jnp.sum(jnp.exp(policy - policy_top), axis=0))
    policy_part = policy - policy_lse
    kl = jnp.sum(jnp.exp(policy_part) * (kl + policy_part - (ref - ref_lse)), axis=0)
    return jnp.stack([ref_lse, policy_lse, kl, jnp.sum(picked, axis=0)])


def device(x, z, y, c):
    return ((x * NZ + z) * NY + y) * NC + c


def along_x(c):
    return [[device(x, z, y, c) for x in range(NX)] for z in range(NZ) for y in range(NY)]


def along_y(c):
    return [[device(x, z, y, c) for y in range(NY)] for z in range(NZ) for x in range(NX)]


def share_plane(block):
    first, second = along_x(0) + along_y(1), along_y(0) + along_x(1)
    block = jnp.broadcast_to(block[None], (4,) + block.shape)
    block = lax.all_to_all(block, VOC, 0, 0, axis_index_groups=first)
    block = jnp.broadcast_to(block[None], (4,) + block.shape)
    return lax.all_to_all(block, VOC, 0, 0, axis_index_groups=second)


def head_kernel(
    core, hidden, own_weight, peer_weight, own_out, peer_out, held, own_held, peer_held, sums, sems
):
    rows, half = hidden.shape[2:]
    tokens, steps = own_out.shape[0], sems.shape[1]
    depth = half // steps

    def copies(step):
        part = pl.ds(step * depth, depth)
        at = pl.ds(pl.multiple_of(core[0] * half + step * depth, depth), depth)
        return [
            pltpu.make_async_copy(
                hidden.at[:, :, :, part], held.at[:, :, :, part], sems.at[0, step]
            ),
            pltpu.make_async_copy(own_weight.at[at, :], own_held.at[part, :], sems.at[1, step]),
            pltpu.make_async_copy(peer_weight.at[at, :], peer_held.at[part, :], sems.at[2, step]),
        ]

    for step in range(steps):
        for copy in copies(step):
            copy.start()
    for step in range(steps):
        for copy in copies(step):
            copy.wait()
        part = pl.ds(step * depth, depth)
        block = held[:, :, :, part].reshape(tokens, depth)
        for i, weight in enumerate((own_held, peer_held)):
            product = jnp.dot(block, weight[part, :], preferred_element_type=F32)
            sums[i] = product if step == 0 else sums[i] + product
    for i in range(4):
        for j in range(4):
            to = jnp.where(core[0] == 0, j * 4 + i, i * 4 + j)
            at = pl.ds(pl.multiple_of(to * rows, rows), rows)
            own_out[at, :] = sums[0, pl.ds((i * 4 + j) * rows, rows), :]
            peer_out[at, :] = sums[1, pl.ds((i * 4 + j) * rows, rows), :]


def head(core, hidden, own_weight, peer_weight):
    half, steps = hidden.shape[-1], 8
    tokens, cols = 16 * hidden.shape[2], own_weight.shape[1]
    vmem, anywhere = pl.BlockSpec(memory_space=pltpu.VMEM), pl.BlockSpec(memory_space=pl.ANY)
    return pl.pallas_call(
        head_kernel,
        in_specs=[pl.BlockSpec(memory_space=pltpu.SMEM), anywhere, anywhere, anywhere],
        out_specs=[vmem, vmem],
        out_shape=[jax.ShapeDtypeStruct((tokens, cols), F32)] * 2,
        scratch_shapes=[
            pltpu.VMEM(hidden.shape, BF16),
            pltpu.VMEM((half, cols), BF16),
            pltpu.VMEM((half, cols), BF16),
            pltpu.VMEM((2, tokens, cols), F32),
            pltpu.SemaphoreType.DMA((3, steps)),
        ],
        compiler_params=pltpu.CompilerParams(vmem_limit_bytes=60 * 2**20),
        cost_estimate=pl.CostEstimate(
            flops=4 * tokens * cols * half,
            bytes_accessed=2 * hidden.size + 4 * half * cols,
            transcendentals=0,
        ),
    )(core.reshape(1).astype(jnp.int32), hidden, own_weight, peer_weight)


def on_device(
    attn_out,
    residual,
    o_weight,
    norm_gain,
    head_weight,
    head_scale,
    policy_logits,
    token_ids,
    lengths,
    loss_mask,
):
    tokens = residual.shape[0]
    rows_x = tokens // NX
    rows = rows_x // NY
    cols = o_weight.shape[1]
    depth = o_weight.shape[0]
    half = D // NC
    vocab_dev = head_weight.shape[1]

    peer_weight = swap_cores(head_weight)
    gain_rows = jnp.concatenate(
        [jnp.stack(pieces(norm_gain)), jnp.zeros((13, cols), BF16)]
    )
    to_x = jnp.concatenate(
        [
            jnp.broadcast_to(o_weight[None], (NX, depth, cols)),
            residual.reshape(NX, rows_x, cols),
            jnp.broadcast_to(gain_rows[None], (NX, 16, cols)),
        ],
        axis=1,
    )
    positions = jnp.arange(tokens, dtype=jnp.int32)
    to_x, me, positions = lax.optimization_barrier((to_x, lax.axis_index(VOC), positions))
    from_x = lax.all_to_all(to_x, "x", 0, 0)
    attn_out, from_x, me = lax.optimization_barrier((attn_out, from_x, me))
    attn = share(attn_out, "z", NZ).reshape(rows_x, depth)
    attn, from_x, me = lax.optimization_barrier((attn, from_x, me))
    c, y = me & 1, (me >> 1) & 3
    all_residual, all_gain = lax.optimization_barrier(
        (
            from_x[:, depth : depth + rows_x],
            join(*(from_x[:, depth + rows_x + i] for i in range(3))),
        )
    )
    terms = jnp.stack(
        [
            jnp.dot(attn, from_x[i, :depth], preferred_element_type=F32)
            for i in range(NX)
        ]
    )
    terms = terms.reshape(NC, NX // NC, NY, rows, cols).transpose(2, 0, 1, 3, 4)
    inputs = (policy_logits, token_ids, lengths, loss_mask, positions)
    terms, inputs = lax.optimization_barrier((terms, inputs))
    policy_logits, token_ids, lengths, loss_mask, positions = inputs
    policy_max = jnp.max(policy_logits, axis=1).astype(F32)
    policy_sum = jnp.sum(jnp.exp(policy_logits.astype(F32) - policy_max[:, None]), axis=1)
    policy_log = jnp.log(policy_sum)
    slots = jnp.arange(lengths.shape[0], dtype=jnp.int32)
    seq_len = jnp.sum(
        jnp.where((positions // RESP)[:, None] == slots[None, :], lengths[None, :], 0), axis=1
    )
    live = jnp.where((positions % RESP < seq_len) & (loss_mask > 0), 1.0, 0.0).astype(F32)
    own_residual = lax.dynamic_slice(
        all_residual, (c * (NX // NC), y * rows, 0), (NX // NC, rows, cols)
    )
    gain = lax.dynamic_slice_in_dim(all_gain, c * (NX // NC), NX // NC, 0)
    terms = lax.all_to_all(terms.reshape(NY * NC, NX // NC, rows, cols), TP, 0, 0)
    terms, own_residual, gain, me, policy_max, policy_sum, policy_log, live, peer_weight = (
        lax.optimization_barrier(
            (terms, own_residual, gain, me, policy_max, policy_sum, policy_log, live, peer_weight)
        )
    )
    stream = own_residual.astype(F32) + jnp.sum(terms, axis=0)
    squares = jnp.sum(stream * stream, axis=(0, 2))
    squares = share(squares[None], ("z", "c"), NZ * NC)
    row_scale = lax.rsqrt(jnp.sum(squares, axis=(0, 1)) / D + 1e-06)
    scaled = (stream * row_scale[:, None] * gain[:, None, :]).astype(BF16)

    to_z = lax.optimization_barrier(scaled.reshape(NX // NC * rows, cols))
    from_z = share(to_z, "z", NZ).reshape(NZ, NX // NC, rows, cols)
    features = from_z.transpose(2, 1, 0, 3).reshape(rows, half)
    hidden, me = lax.optimization_barrier((share_plane(features), me))
    own_logits, peer_logits = head(me & 1, hidden, head_weight, peer_weight)
    raw_logits = own_logits + swap_cores(peer_logits)
    ref_logits = raw_logits * head_scale[None, :]

    policy = policy_logits.astype(F32)
    columns = me * vocab_dev + jnp.arange(vocab_dev, dtype=jnp.int32)
    picked = jnp.sum(
        jnp.where(token_ids[:, None] == columns[None, :], ref_logits, 0.0), axis=1
    )
    ref_max = jnp.max(ref_logits, axis=1)
    ref_down = ref_logits - ref_max[:, None]
    policy_down = policy - policy_max[:, None]
    policy_exp = jnp.exp(policy_down)
    ref_log = jnp.log(jnp.sum(jnp.exp(ref_down), axis=1))
    kl_part = jnp.sum(policy_exp * (policy_down - ref_down), axis=1) / policy_sum
    kl_part = kl_part - policy_log + ref_log
    stats = jnp.stack([ref_max + ref_log, policy_max + policy_log, kl_part, picked])
    stats = combine(share(stats, ("x", "y", "c"), NX * NY * NC))
    ref_lse, policy_lse, kl_raw, picked = combine(share(stats, "z", NZ))
    ref_logp = ref_logits - ref_lse[:, None]
    policy_logp = policy - policy_lse[:, None]
    grad_policy = (
        live[:, None] * jnp.exp(policy_logp) * (policy_logp - ref_logp - kl_raw[:, None])
    ).astype(BF16)
    return (grad_policy, picked - ref_lse, live * kl_raw)


def solution(mesh):
    fine = Mesh(mesh.devices.reshape(NX, NZ, NY, NC), VOC)
    in_specs = (
        P(PIPE, TP),
        P(None, PIPE),
        P(TP, PIPE),
        P(PIPE),
        P(None, VOC),
        P(VOC),
        P(None, VOC),
        P(),
        P(),
        P(),
    )
    out_specs = (P(None, VOC), P(), P())
    return jax.shard_map(
        on_device, mesh=fine, in_specs=in_specs, out_specs=out_specs, check_vma=False
    )
```
